512 devices in a mesh: tm: 64 (over z, y), space: 8 (over x, core).
Axes of the slice: x: 4, y: 4, z: 16, core: 2. Of those that a mesh axis runs over, the one named last changes fastest.
Arguments:
- frames: bfloat16 [256, 256, 4096], P('tm', 'space'), may hold values from -6 to 6
- norm_gain: float32 [4096], replicated, may hold values from 0.1 to 1.9
- w_qkv: bfloat16 [4096, 3, 2048], P('tm', None, 'space'), may hold values from -2 to 2
Outputs:
- attended: bfloat16 [256, 256, 2048], P('tm', None, 'space')
The draws below stay inside these ranges and needn't reach their ends.
All inputs are finite; a program needn't handle non-finite values.
Results may differ from the reference program's by a relative error of at most 0.0068.
Values may be sent and summed in bfloat16 or wider, within the bound.
No kernel may reach another device: no remote copies, remote signals or barrier semaphores. Data moves between devices by JAX's collectives and lax.ppermute only.
A program may use at most 64 MiB of HBM per device.

```python
import jax
import jax.numpy as jnp
from jax import lax

D = 4096
HEADS = 16
HEAD = 128
PATCHES = 256
FRAMES = 256
HD = 2048


def draw_w_qkv(key, part):
    key = jax.random.fold_in(key, 11)
    key_base = jax.random.fold_in(key, 0)
    base_draw = jax.random.normal(key_base, (D, 3, HD), jnp.float32) * D ** (-0.5)
    return jnp.clip(base_draw, -2.0, 2.0).astype(jnp.bfloat16)


def shard_levels(own_key, shape, cuts, low, top_value):
    level = 1.0
    for dim, shards_of in cuts:
        draws = jax.random.uniform(jax.random.fold_in(jax.random.fold_in(own_key, 6), dim), (shards_of,), jnp.float32, low / len(cuts), top_value / len(cuts))
        level = level * jnp.repeat(jnp.exp(draws), shape[dim] // shards_of).reshape((-1,) + (1,) * (len(shape) - 1 - dim))
    return level


def noise(rng, shape, scale, reach, shards=(), kind=jnp.bfloat16):
    array = scale * jax.random.normal(rng, shape, jnp.float32)
    if shards:
        array = array * shard_levels(rng, shape, shards, -0.22, 0.18)
    return jnp.clip(array, -reach, reach).astype(kind)


def setup_inputs(seed: int = 0) -> dict:
    splits = jax.random.split(jax.random.key(seed), 4)
    return {
        "frames": noise(splits[0], (FRAMES, PATCHES, D), 1.0, 6.0, ((0, 64), (1, 8))),
        "norm_gain": jnp.clip(1.0 + 0.18 * jax.random.normal(splits[1], (D,), jnp.float32), 0.1, 1.9),
        "w_qkv": draw_w_qkv(jax.random.fold_in(splits[3], 71), 0),
    }


def attend(query, key_block, values):
    score_scale = HEAD ** (-0.5)
    scores = jnp.einsum('fha,gha->hfg', query.astype(jnp.float32), key_block.astype(jnp.float32)) * score_scale
    row_index = lax.broadcasted_iota(jnp.int32, scores.shape, 1)
    col_index = lax.broadcasted_iota(jnp.int32, scores.shape, 2)
    scores = jnp.where(col_index <= row_index, scores, -jnp.inf)
    row_max = lax.optimization_barrier(jnp.max(scores, axis=-1, keepdims=True))
    exp_scores = jnp.exp(scores - row_max)
    attn_weights = (exp_scores / lax.optimization_barrier(jnp.sum(exp_scores, axis=-1, keepdims=True))).astype(jnp.bfloat16)
    mixed = jnp.einsum('hfg,gha->fha', attn_weights.astype(jnp.float32), values.astype(jnp.float32))
    return mixed.astype(jnp.bfloat16)

def reference(frames, norm_gain, w_qkv):
    weights = w_qkv.reshape(D, 3 * HD)

    def one_patch(tokens):
        widened = tokens.astype(jnp.float32)
        mean_square = lax.optimization_barrier(jnp.mean(widened * widened, axis=-1, keepdims=True))
        normed = (widened * lax.rsqrt(mean_square + 1e-05) * norm_gain).astype(jnp.bfloat16)
        projected = jnp.dot(normed, weights, preferred_element_type=jnp.float32).astype(jnp.bfloat16)
        projected = projected.reshape(FRAMES, 3, HEADS, HEAD)
        result = attend(projected[:, 0], projected[:, 1], projected[:, 2])
        return result.reshape(FRAMES, HD)
    per_patch = lax.map(one_patch, jnp.swapaxes(frames, 0, 1))
    return jnp.swapaxes(per_patch, 0, 1)
```

```python
import jax
import jax.numpy as jnp
from jax import lax
from jax.experimental import pallas as pl
from jax.experimental.pallas import tpu as pltpu
from jax.sharding import Mesh, PartitionSpec as P

BF, F32 = jnp.bfloat16, jnp.float32
Z, Y, X, C = 16, 4, 4, 2
D, HEAD = 4096, 128
VMEM = pltpu.VMEM


def iota(shape, dim):
    return lax.broadcasted_iota(jnp.int32, shape, dim)


def one_hot(source):
    return lambda n, m: jnp.where(source(iota((n, m), 0)) == iota((n, m), 1), 1.0, 0.0).astype(BF)


def pick(matrix, rows):
    return jnp.dot(matrix, rows, preferred_element_type=F32)


def normalize_kernel(frames_ref, gain_ref, out_ref):
    rows = frames_ref[...].reshape(128, D).astype(F32)
    scale = lax.rsqrt(jnp.mean(rows * rows, axis=-1, keepdims=True) + 1e-05)
    shuffle = one_hot(lambda i: (i & 3) * 32 + (i >> 3) * 2 + ((i >> 2) & 1))(128, 128)
    spread = one_hot(lambda i: ((i >> 6) & 3) * 128 + (i >> 8) * 64 + (i & 63))(512, 512)
    for j in range(8):
        cut = slice(512 * j, 512 * (j + 1))
        normed = (rows[:, cut] * scale * gain_ref[:, cut]).astype(BF)
        moved = pick(pick(shuffle, normed).astype(BF), spread).astype(BF)
        for y in range(Y):
            out_ref[:, 1024 * y + 128 * j : 1024 * y + 128 * (j + 1)] = moved[:, 128 * y : 128 * (y + 1)]


def project_kernel(y_ref, tokens_ref, own_ref, below_ref, above_ref, far_low_ref, far_high_ref, out_ref):
    y = y_ref[0]

    def slab(where, width):
        return tokens_ref[:, pl.ds(pl.multiple_of(where, 512), width)]

    own = slab(y * 1024, 1024)
    below = slab(((y + 3) & 3) * 1024, 1024)
    above = slab(((y + 1) & 3) * 1024, 1024)
    far_low = slab(((y + 2) & 3) * 1024, 512)
    far_high = slab(((y + 2) & 3) * 1024 + 512, 512)
    for c in range(3):
        total = None
        for part, ref in (
            (own, own_ref), (below, below_ref), (above, above_ref), (far_low, far_low_ref), (far_high, far_high_ref),
        ):
            weights = ref[:, c].reshape(ref.shape[0] * 64, 256)
            term = jnp.dot(part, weights, preferred_element_type=F32)
            total = term if total is None else total + term
        out_ref[:, 256 * c : 256 * (c + 1)] = total.astype(BF)


def attend_kernel(qkv_ref, out_ref):
    def source(i):
        return ((i >> 2) & 3) * 128 + ((i >> 4) & 15) * 8 + (i >> 8) * 4 + (i & 3)

    order = one_hot(source)(512, 512)
    back = one_hot(lambda i: ((i >> 2) & 1) * 256 + (i >> 3) * 4 + (i & 3))(512, 512)
    keep = iota((256, 256), 1) <= iota((256, 256), 0)
    halves = []
    for c in range(C):
        rows = pick(order, qkv_ref[:, 128 * c : 128 * (c + 1)].reshape(512, 768)).astype(BF)
        patches = []
        for p in range(2):
            mine = rows[256 * p : 256 * (p + 1)]
            heads = []
            for h in range(2):
                query, key, value = (mine[:, 256 * k + 128 * h : 256 * k + 128 * (h + 1)] for k in range(3))
                scores = lax.dot_general(query, key, (((1,), (1,)), ((), ())), preferred_element_type=F32) * HEAD**-0.5
                scores = jnp.where(keep, scores, -jnp.inf)
                grown = jnp.exp(scores - jnp.max(scores, axis=-1, keepdims=True))
                probs = (grown / jnp.sum(grown, axis=-1, keepdims=True)).astype(BF)
                heads.append(jnp.dot(probs, value, preferred_element_type=F32).astype(BF))
            patches.append(jnp.concatenate(heads, axis=1))
        halves.append(pick(back, jnp.concatenate(patches, axis=0)).reshape(64, 8, 256))
    out_ref[...] = jnp.concatenate(halves, axis=1).astype(BF)


def place_kernel(mixed_ref, out_ref):
    order = one_hot(lambda i: ((i >> 1) & 15) * 16 + ((i >> 5) & 1) * 8 + (i & 1) * 4 + (i >> 6))(256, 256)
    for y in range(Y):
        rows = pick(order, mixed_ref[:, y].reshape(256, 256)).astype(BF)
        for f in range(4):
            out_ref[f, 64 * y : 64 * (y + 1)] = rows[64 * f : 64 * (f + 1)]


def whole():
    return pl.BlockSpec(memory_space=VMEM)


def call(kernel, out_shape, *operands, **kwargs):
    return pl.pallas_call(
        kernel,
        out_shape=jax.ShapeDtypeStruct(out_shape, BF),
        in_specs=[whole()] * len(operands),
        out_specs=whole(),
        compiler_params=pltpu.CompilerParams(vmem_limit_bytes=40 * 2**20),
        **kwargs,
    )(*operands)


def shift(x, axis, by):
    n = {"z": Z, "y": Y, "x": X, "c": C}[axis]
    return lax.ppermute(x, axis, [(i, (i + by) % n) for i in range(n)])


def shards(frames, norm_gain, w_qkv):
    weights = lax.all_gather(jnp.transpose(w_qkv, (1, 0, 2)), "z", axis=0)
    packed = call(normalize_kernel, (128, D), frames, norm_gain.reshape(1, D))
    tokens = lax.all_to_all(packed.reshape(Z, 8, D), "z", 0, 0, tiled=True).reshape(128, D)
    below = shift(weights, "y", 1)
    above = shift(weights, "y", -1)
    far_low = shift(below[:8], "y", 1)
    far_high = shift(above[8:], "y", -1)
    gathered = lax.all_gather(tokens, ("x", "c"), axis=0, tiled=True)
    here = lax.axis_index("y").astype(jnp.int32).reshape(1)
    rows = 256
    fixed = lambda k: pl.BlockSpec((k, 3, 64, 256), lambda i: (0, 0, 0, 0))
    qkv = pl.pallas_call(
        project_kernel,
        grid=(1024 // rows,),
        out_shape=jax.ShapeDtypeStruct((1024, 768), BF),
        in_specs=[pl.BlockSpec(memory_space=pltpu.SMEM), pl.BlockSpec((rows, D), lambda i: (i, 0)),
                  fixed(16), fixed(16), fixed(16), fixed(8), fixed(8)],
        out_specs=pl.BlockSpec((rows, 768), lambda i: (i, 0)),
        compiler_params=pltpu.CompilerParams(vmem_limit_bytes=48 * 2**20),
    )(here, gathered, weights, below, above, far_low, far_high)
    qkv = lax.all_to_all(qkv.reshape(Y, 256, 768), "y", 0, 0, tiled=True)
    mixed = call(attend_kernel, (64, 16, 256), qkv)
    mixed = lax.all_to_all(mixed, ("z", "y"), 0, 0, tiled=True)
    return call(place_kernel, (4, 256, 256), mixed.reshape(Z, Y, 16, 256))


def solution(mesh):
    grid = Mesh(mesh.devices.reshape(Z, Y, X, C), ("z", "y", "x", "c"))
    rows, columns = ("z", "y"), ("x", "c")
    return jax.shard_map(
        shards, mesh=grid, in_specs=(P(rows, columns, None), P(), P(rows, None, columns)),
        out_specs=P(rows, None, columns), check_vma=False,
    )
```

```python
import jax
import jax.numpy as jnp
from jax import lax
from jax.experimental import pallas as pl
from jax.experimental.pallas import tpu as pltpu
from jax.sharding import Mesh, PartitionSpec as P

BF, F32 = jnp.bfloat16, jnp.float32
Z, Y, X, C = 16, 4, 4, 2
D, HEAD = 4096, 128
VMEM = pltpu.VMEM


def iota(shape, dim):
    return lax.broadcasted_iota(jnp.int32, shape, dim)


def one_hot(source):
    return lambda n, m: jnp.where(source(iota((n, m), 0)) == iota((n, m), 1), 1.0, 0.0).astype(BF)


def pick(matrix, rows):
    return jnp.dot(matrix, rows, preferred_element_type=F32)


def normalize_kernel(frames_ref, gain_ref, out_ref):
    rows = frames_ref[...].reshape(128, D).astype(F32)
    scale = lax.rsqrt(jnp.mean(rows * rows, axis=-1, keepdims=True) + 1e-05)
    shuffle = one_hot(lambda i: (i & 3) * 32 + (i >> 3) * 2 + ((i >> 2) & 1))(128, 128)
    for j in range(8):
        cut = slice(512 * j, 512 * (j + 1))
        normed = (rows[:, cut] * scale * gain_ref[:, cut]).astype(BF)
        out_ref[:, cut] = pick(shuffle, normed).astype(BF)


def ready_kernel(weights_ref, out_ref):
    out_ref[...] = jnp.zeros_like(out_ref)


def spread_kernel(tokens_ref, ready_ref, out_ref):
    spread = one_hot(lambda i: ((i >> 6) & 3) * 128 + (i >> 8) * 64 + (i & 63))(512, 512)
    for j in range(8):
        moved = pick(tokens_ref[:, 512 * j : 512 * (j + 1)], spread).astype(BF)
        for y in range(Y):
            out_ref[:, 1024 * y + 128 * j : 1024 * y + 128 * (j + 1)] = moved[:, 128 * y : 128 * (y + 1)]


def project_kernel(y_ref, tokens_ref, own_ref, below_ref, above_ref, far_low_ref, far_high_ref, out_ref):
    y = y_ref[0]

    def slab(where, width):
        return tokens_ref[:, pl.ds(pl.multiple_of(where, 512), width)]

    own = slab(y * 1024, 1024)
    below = slab(((y + 3) & 3) * 1024, 1024)
    above = slab(((y + 1) & 3) * 1024, 1024)
    far_low = slab(((y + 2) & 3) * 1024, 512)
    far_high = slab(((y + 2) & 3) * 1024 + 512, 512)
    for c in range(3):
        total = None
        for part, ref in (
            (own, own_ref), (below, below_ref), (above, above_ref), (far_low, far_low_ref), (far_high, far_high_ref),
        ):
            weights = ref[:, c].reshape(ref.shape[0] * 64, 256)
            term = jnp.dot(part, weights, preferred_element_type=F32)
            total = term if total is None else total + term
        out_ref[:, 256 * c : 256 * (c + 1)] = total.astype(BF)


def attend_kernel(qkv_ref, out_ref):
    def source(i):
        return ((i >> 2) & 3) * 128 + ((i >> 4) & 15) * 8 + (i >> 8) * 4 + (i & 3)

    order = one_hot(source)(512, 512)
    back = one_hot(lambda i: ((i >> 2) & 1) * 256 + (i >> 3) * 4 + (i & 3))(512, 512)
    keep = iota((256, 256), 1) <= iota((256, 256), 0)
    halves = []
    for c in range(C):
        rows = pick(order, qkv_ref[:, 128 * c : 128 * (c + 1)].reshape(512, 768)).astype(BF)
        patches = []
        for p in range(2):
            mine = rows[256 * p : 256 * (p + 1)]
            heads = []
            for h in range(2):
                query, key, value = (mine[:, 256 * k + 128 * h : 256 * k + 128 * (h + 1)] for k in range(3))
                scores = lax.dot_general(query, key, (((1,), (1,)), ((), ())), preferred_element_type=F32) * HEAD**-0.5
                scores = jnp.where(keep, scores, -jnp.inf)
                grown = jnp.exp(scores - jnp.max(scores, axis=-1, keepdims=True))
                probs = (grown / jnp.sum(grown, axis=-1, keepdims=True)).astype(BF)
                heads.append(jnp.dot(probs, value, preferred_element_type=F32).astype(BF))
            patches.append(jnp.concatenate(heads, axis=1))
        halves.append(pick(back, jnp.concatenate(patches, axis=0)).reshape(64, 8, 256))
    out_ref[...] = jnp.concatenate(halves, axis=1).astype(BF)


def place_kernel(mixed_ref, out_ref):
    order = one_hot(lambda i: ((i >> 1) & 15) * 16 + ((i >> 5) & 1) * 8 + (i & 1) * 4 + (i >> 6))(256, 256)
    for y in range(Y):
        rows = pick(order, mixed_ref[:, y].reshape(256, 256)).astype(BF)
        for f in range(4):
            out_ref[f, 64 * y : 64 * (y + 1)] = rows[64 * f : 64 * (f + 1)]


def whole():
    return pl.BlockSpec(memory_space=VMEM)


def call(kernel, out_shape, *operands, **kwargs):
    return pl.pallas_call(
        kernel,
        out_shape=jax.ShapeDtypeStruct(out_shape, BF),
        in_specs=[whole()] * len(operands),
        out_specs=whole(),
        compiler_params=pltpu.CompilerParams(vmem_limit_bytes=40 * 2**20),
        **kwargs,
    )(*operands)


def shift(x, axis, by):
    n = {"z": Z, "y": Y, "x": X, "c": C}[axis]
    return lax.ppermute(x, axis, [(i, (i + by) % n) for i in range(n)])


def shards(frames, norm_gain, w_qkv):
    weights = lax.all_gather(jnp.transpose(w_qkv, (1, 0, 2)), "z", axis=0)
    packed = call(normalize_kernel, (128, D), frames, norm_gain.reshape(1, D))
    tokens = lax.all_to_all(packed.reshape(Z, 8, D), "z", 0, 0, tiled=True).reshape(128, D)
    ready = pl.pallas_call(
        ready_kernel,
        out_shape=jax.ShapeDtypeStruct((16, 128), BF),
        in_specs=[pl.BlockSpec(memory_space=pl.ANY)],
        out_specs=whole(),
        cost_estimate=pl.CostEstimate(flops=10**11, bytes_accessed=0, transcendentals=0),
    )(weights)
    tokens = call(spread_kernel, (128, D), tokens, ready)
    below = shift(weights, "y", 1)
    above = shift(weights, "y", -1)
    far_low = shift(below[:8], "y", 1)
    far_high = shift(above[8:], "y", -1)
    gathered = lax.all_gather(tokens, ("x", "c"), axis=0, tiled=True)
    here = lax.axis_index("y").astype(jnp.int32).reshape(1)
    rows = 256
    fixed = lambda k: pl.BlockSpec((k, 3, 64, 256), lambda i: (0, 0, 0, 0))
    qkv = pl.pallas_call(
        project_kernel,
        grid=(1024 // rows,),
        out_shape=jax.ShapeDtypeStruct((1024, 768), BF),
        in_specs=[pl.BlockSpec(memory_space=pltpu.SMEM), pl.BlockSpec((rows, D), lambda i: (i, 0)),
                  fixed(16), fixed(16), fixed(16), fixed(8), fixed(8)],
        out_specs=pl.BlockSpec((rows, 768), lambda i: (i, 0)),
        compiler_params=pltpu.CompilerParams(vmem_limit_bytes=48 * 2**20),
    )(here, gathered, weights, below, above, far_low, far_high)
    qkv = lax.all_to_all(qkv.reshape(Y, 256, 768), "y", 0, 0, tiled=True)
    mixed = call(attend_kernel, (64, 16, 256), qkv)
    mixed = lax.all_to_all(mixed, ("z", "y"), 0, 0, tiled=True)
    return call(place_kernel, (4, 256, 256), mixed.reshape(Z, Y, 16, 256))


def solution(mesh):
    grid = Mesh(mesh.devices.reshape(Z, Y, X, C), ("z", "y", "x", "c"))
    rows, columns = ("z", "y"), ("x", "c")
    return jax.shard_map(
        shards, mesh=grid, in_specs=(P(rows, columns, None), P(), P(rows, None, columns)),
        out_specs=P(rows, None, columns), check_vma=False,
    )
```

```python
import jax
import jax.numpy as jnp
from jax import lax
from jax.experimental import pallas as pl
from jax.experimental.pallas import tpu as pltpu
from jax.sharding import Mesh, PartitionSpec as P

BF, F32 = jnp.bfloat16, jnp.float32
Z, Y, X, C = 16, 4, 4, 2
D, HEAD = 4096, 128
VMEM = pltpu.VMEM


def iota(shape, dim):
    return lax.broadcasted_iota(jnp.int32, shape, dim)


def one_hot(source, n, m):
    return jnp.where(source(iota((n, m), 0)) == iota((n, m), 1), 1.0, 0.0).astype(BF)


def pick(matrix, rows):
    return jnp.dot(matrix, rows, preferred_element_type=F32).astype(BF)


def normalize_kernel(frames_ref, gain_ref, out_ref):
    rows = frames_ref[...].reshape(128, D).astype(F32)
    scale = lax.rsqrt(jnp.mean(rows * rows, axis=-1, keepdims=True) + 1e-05)
    shuffle = one_hot(
        lambda i: ((i >> 2) & 1) * 128 + ((i >> 4) & 3) * 32 + (i >> 6) * 8 + ((i >> 3) & 1) * 4 + (i & 3), 256, 256
    )
    for j in range(4):
        cuts = [slice(2048 * half + 512 * j, 2048 * half + 512 * (j + 1)) for half in range(2)]
        normed = jnp.concatenate([(rows[:, cut] * scale * gain_ref[:, cut]).astype(BF) for cut in cuts], axis=0)
        out_ref[:, 512 * j : 512 * (j + 1)] = pick(shuffle, normed)


def route_kernel(in_ref, out_ref):
    order = one_hot(
        lambda i: ((i >> 2) & 3) * 64 + (i >> 5) * 8 + ((i >> 1) & 1) * 4 + ((i >> 4) & 1) * 2 + (i & 1), 256, 256
    )
    for j in range(4):
        cut = slice(512 * j, 512 * (j + 1))
        out_ref[:, cut] = pick(order, in_ref[:, cut])


def ready_kernel(weights_ref, out_ref):
    out_ref[...] = jnp.zeros_like(out_ref)


def spread_kernel(tokens_ref, ready_ref, out_ref):
    spread = one_hot(lambda i: ((i >> 6) & 3) * 128 + (i >> 8) * 64 + (i & 63), 512, 512)
    for half in range(2):
        order = one_hot(lambda i: (i & 63) * 4 + half * 2 + (i >> 6), 128, 256)
        for j in range(4):
            moved = pick(pick(order, tokens_ref[:, 512 * j : 512 * (j + 1)]), spread)
            for y in range(Y):
                start = 1024 * y + 128 * (4 * half + j)
                out_ref[:, start : start + 128] = moved[:, 128 * y : 128 * (y + 1)]


def attend(query, key, value, keep):
    scores = lax.dot_general(query, key, (((1,), (1,)), ((), ())), preferred_element_type=F32) * HEAD**-0.5
    scores = jnp.where(keep, scores, -jnp.inf)
    grown = jnp.exp(scores - jnp.max(scores, axis=-1, keepdims=True))
    probs = (grown / jnp.sum(grown, axis=-1, keepdims=True)).astype(BF)
    return jnp.dot(probs, value, preferred_element_type=F32).astype(BF)


def patch_kernel(y_ref, tokens_ref, own_ref, below_ref, above_ref, far_low_ref, far_high_ref, out_ref, mixed_ref):
    step = pl.program_id(0)
    y = y_ref[0]

    def slab(where, width):
        return tokens_ref[:, 0, 0, :, pl.ds(pl.multiple_of(where, 512), width)].reshape(256, width)

    pairs = (
        (slab(y * 1024, 1024), own_ref),
        (slab(((y + 3) & 3) * 1024, 1024), below_ref),
        (slab(((y + 1) & 3) * 1024, 1024), above_ref),
        (slab(((y + 2) & 3) * 1024, 512), far_low_ref),
        (slab(((y + 2) & 3) * 1024 + 512, 512), far_high_ref),
    )
    qkv = []
    for c in range(3):
        total = None
        for part, ref in pairs:
            term = jnp.dot(part, ref[:, c].reshape(ref.shape[0] * 64, 256), preferred_element_type=F32)
            total = term if total is None else total + term
        qkv.append(total.astype(BF))
    frame = lambda i: (i & 63) * 4 + (i >> 6)
    keep = frame(iota((256, 256), 1)) <= frame(iota((256, 256), 0))
    heads = [attend(*(part[:, HEAD * h : HEAD * (h + 1)] for part in qkv), keep) for h in range(2)]
    mixed_ref[step] = jnp.concatenate(heads, axis=1)

    @pl.when(step == 3)
    def _():
        order = one_hot(lambda i: (i & 15) * 16 + (i >> 4), 256, 256)
        for k in range(4):
            rows = [mixed_ref[g, 64 * f + 16 * k : 64 * f + 16 * (k + 1)] for g in range(4) for f in range(4)]
            out_ref[16 * k : 16 * (k + 1)] = pick(order, jnp.concatenate(rows, axis=0)).reshape(16, 16, 256)


def place_kernel(mixed_ref, out_ref):
    order = one_hot(
        lambda i: ((i >> 1) & 1) * 64 + ((i >> 3) & 3) * 16 + ((i >> 2) & 1) * 8 + (i & 1) * 4 + (i >> 5), 128, 128
    )
    for g in range(8):
        rows = pick(order, mixed_ref[8 * g : 8 * (g + 1)].reshape(128, 256))
        for f in range(4):
            out_ref[f, 32 * g : 32 * (g + 1)] = rows[32 * f : 32 * (f + 1)]


def whole():
    return pl.BlockSpec(memory_space=VMEM)


def call(kernel, out_shape, *operands):
    return pl.pallas_call(
        kernel,
        out_shape=jax.ShapeDtypeStruct(out_shape, BF),
        in_specs=[whole()] * len(operands),
        out_specs=whole(),
        compiler_params=pltpu.CompilerParams(vmem_limit_bytes=40 * 2**20),
    )(*operands)


def shift(x, axis, by):
    n = {"z": Z, "y": Y, "x": X, "c": C}[axis]
    return lax.ppermute(x, axis, [(i, (i + by) % n) for i in range(n)])


def project_and_attend(tokens, here, *weights):
    fixed = lambda w: pl.BlockSpec(w.shape, lambda i: (0, 0, 0, 0))
    return pl.pallas_call(
        patch_kernel,
        grid=(4,),
        out_shape=jax.ShapeDtypeStruct((64, 16, 256), BF),
        in_specs=[pl.BlockSpec(memory_space=pltpu.SMEM),
                  pl.BlockSpec((4, 1, 1, 64, D), lambda i: (0, i // 2, i % 2, 0, 0))] + [fixed(w) for w in weights],
        out_specs=pl.BlockSpec((64, 16, 256), lambda i: (0, 0, 0)),
        scratch_shapes=[VMEM((4, 256, 256), BF)],
        compiler_params=pltpu.CompilerParams(vmem_limit_bytes=48 * 2**20),
    )(here, tokens, *weights)


def shards(frames, norm_gain, w_qkv):
    weights = lax.all_gather(jnp.transpose(w_qkv, (1, 0, 2)), "z", axis=0)
    packed = call(normalize_kernel, (256, 2048), frames, norm_gain.reshape(1, D))
    spread = lax.all_to_all(packed.reshape(32, 8, 2048), ("y", "x", "c"), 0, 0, tiled=True)
    routed = call(route_kernel, (256, 2048), spread.reshape(256, 2048))
    tokens = lax.all_to_all(routed.reshape(Z, 16, 2048), "z", 0, 0, tiled=True).reshape(256, 2048)
    ready = pl.pallas_call(
        ready_kernel,
        out_shape=jax.ShapeDtypeStruct((16, 128), BF),
        in_specs=[pl.BlockSpec(memory_space=pl.ANY)],
        out_specs=whole(),
        cost_estimate=pl.CostEstimate(flops=10**11, bytes_accessed=0, transcendentals=0),
    )(weights)
    tokens = call(spread_kernel, (128, D), tokens, ready)
    below = shift(weights, "y", 1)
    above = shift(weights, "y", -1)
    far_low = shift(below[:8], "y", 1)
    far_high = shift(above[8:], "y", -1)
    gathered = lax.all_gather(tokens, ("x", "c"), axis=0).reshape(4, 2, 2, 64, D)
    here = lax.axis_index("y").astype(jnp.int32).reshape(1)
    mixed = project_and_attend(gathered, here, weights, below, above, far_low, far_high)
    mixed = lax.all_to_all(mixed, ("z", "y"), 0, 0, tiled=True)
    return call(place_kernel, (4, 256, 256), mixed)


def solution(mesh):
    grid = Mesh(mesh.devices.reshape(Z, Y, X, C), ("z", "y", "x", "c"))
    rows, columns = ("z", "y"), ("x", "c")
    return jax.shard_map(
        shards, mesh=grid, in_specs=(P(rows, columns, None), P(), P(rows, None, columns)),
        out_specs=P(rows, None, columns), check_vma=False,
    )
```

```python
import jax
import jax.numpy as jnp
from jax import lax
from jax.experimental import pallas as pl
from jax.experimental.pallas import tpu as pltpu
from jax.sharding import Mesh, PartitionSpec as P

BF, F32 = jnp.bfloat16, jnp.float32
Z, Y, X, C = 16, 4, 4, 2
D, HEAD = 4096, 128
VMEM = pltpu.VMEM


def iota(shape, dim):
    return lax.broadcasted_iota(jnp.int32, shape, dim)


def one_hot(source, n, m):
    return jnp.where(source(iota((n, m), 0)) == iota((n, m), 1), 1.0, 0.0).astype(BF)


def pick(matrix, rows):
    return jnp.dot(matrix, rows, preferred_element_type=F32).astype(BF)


def normalize_kernel(frames_ref, gain_ref, out_ref):
    rows = frames_ref[...].reshape(128, D).astype(F32)
    scale = lax.rsqrt(jnp.mean(rows * rows, axis=-1, keepdims=True) + 1e-05)
    shuffle = one_hot(lambda i: (((i >> 4) & 1) * 2 + (i & 1)) * 32 + (i >> 5) * 8 + ((i >> 1) & 7), 128, 128)
    for j in range(8):
        cut = slice(512 * j, 512 * (j + 1))
        out_ref[:, cut] = pick(shuffle, (rows[:, cut] * scale * gain_ref[:, cut]).astype(BF))


def route_kernel(in_ref, out_ref):
    order = one_hot(lambda i: ((i >> 1) & 3) * 32 + (i >> 3) * 2 + (i & 1), 128, 128)
    for j in range(8):
        cut = slice(512 * j, 512 * (j + 1))
        out_ref[:, cut] = pick(order, in_ref[:, cut])


def stack_kernel(low_ref, high_ref, after_ref, out_ref):
    out_ref[:64] = low_ref[...]
    out_ref[64:] = high_ref[...]


def project(token_refs, weights_ref):
    totals = [None] * 3
    for k in range(4):
        cut = slice(1024 * k, 1024 * (k + 1))
        part = jnp.concatenate([ref[:, cut] for ref in token_refs], axis=0)
        for c in range(3):
            weights = weights_ref[4 * k : 4 * (k + 1), :, c].reshape(1024, 256)
            term = jnp.dot(part, weights, preferred_element_type=F32)
            totals[c] = term if totals[c] is None else totals[c] + term
    return [total.astype(BF) for total in totals]


def attend(qkv, patches, core):
    def frame(i):
        return ((i & 127) >> 1) * 4 + ((i >> 7) ^ core) * 2 + (i & 1)

    keep = frame(iota((256, 256), 1)) <= frame(iota((256, 256), 0))
    scale = HEAD**-0.5 * 1.4426950408889634
    across = (((1,), (1,)), ((), ()))
    mixed = []
    for p in range(patches):
        units = [[part[256 * p : 256 * (p + 1), HEAD * h : HEAD * (h + 1)] for part in qkv] for h in range(2)]
        scores = [lax.dot_general(q, k, across, preferred_element_type=F32) * scale for q, k, _ in units]
        scores = [jnp.where(keep, s, -jnp.inf) for s in scores]
        grown = [jnp.exp2(s - jnp.max(s, axis=-1, keepdims=True)) for s in scores]
        probs = [(g * (1.0 / jnp.sum(g, axis=-1, keepdims=True))).astype(BF) for g in grown]
        heads = [jnp.dot(w, v, preferred_element_type=F32).astype(BF) for w, (_, _, v) in zip(probs, units)]
        mixed.append(jnp.concatenate(heads, axis=1))
    return mixed


def near_kernel(place_ref, *refs):
    *token_refs, weights_ref, out_ref = refs
    for p, mixed in enumerate(attend(project(token_refs, weights_ref), 3, place_ref[1])):
        out_ref[256 * p : 256 * (p + 1)] = mixed


def far_kernel(place_ref, near_ref, far_ref, other_far_ref, weights_ref, out_ref):
    core = place_ref[1]
    (far,) = attend(project((far_ref, other_far_ref), weights_ref), 1, core)
    def source(i):
        return ((i >> 2) & 3) * 64 + (((i >> 1) & 1) ^ core) * 32 + (i >> 4) * 2 + (i & 1)

    order = one_hot(source, 256, 256)
    for k in range(4):
        cuts = [near_ref[128 * g + 32 * k : 128 * g + 32 * (k + 1)] for g in range(6)]
        cuts += [far[128 * g + 32 * k : 128 * g + 32 * (k + 1)] for g in range(2)]
        out_ref[16 * k : 16 * (k + 1)] = pick(order, jnp.concatenate(cuts, axis=0)).reshape(16, 16, 256)


def place_kernel(place_ref, mixed_ref, out_ref):
    def source(i):
        ahead = (((i >> 5) & 3) - place_ref[0]) & 3
        slot = jnp.where(ahead == 0, 0, jnp.where(ahead == 3, 1, ahead + 1))
        return (i & 7) * 64 + ((i >> 3) & 3) * 16 + slot * 4 + (i >> 7)

    order = one_hot(source, 512, 512)
    for core in range(C):
        rows = pick(order, mixed_ref[32 * core : 32 * (core + 1)].reshape(512, 256))
        for f in range(4):
            for x in range(X):
                out_ref[f, 64 * x + 32 * core : 64 * x + 32 * (core + 1)] = rows[128 * f + 32 * x : 128 * f + 32 * (x + 1)]


def call(kernel, out_shape, *operands, flops=10**7, far=()):
    def spec(i, operand):
        return pl.BlockSpec(memory_space=pltpu.SMEM if operand.dtype == jnp.int32 else pl.ANY if i in far else VMEM)

    return pl.pallas_call(
        kernel,
        out_shape=jax.ShapeDtypeStruct(out_shape, BF),
        in_specs=[spec(i, operand) for i, operand in enumerate(operands)],
        out_specs=pl.BlockSpec(memory_space=VMEM),
        compiler_params=pltpu.CompilerParams(vmem_limit_bytes=40 * 2**20),
        cost_estimate=pl.CostEstimate(flops=flops, bytes_accessed=2**21, transcendentals=0),
    )(*operands)


def shift(x, axis, by):
    n = {"z": Z, "y": Y, "x": X, "c": C}[axis]
    return lax.ppermute(x, axis, [(i, (i + by) % n) for i in range(n)])


def shards(frames, norm_gain, w_qkv):
    weights = jnp.broadcast_to(jnp.transpose(w_qkv, (1, 0, 2)), (Y, 3, 64, 256))
    weights = lax.all_to_all(weights, "y", 0, 0, tiled=True)
    weights = lax.all_gather(weights, "z", axis=0)
    packed = call(normalize_kernel, (128, D), frames, norm_gain.reshape(1, D))
    spread = lax.all_to_all(packed.reshape(8, 16, D), ("y", "c"), 0, 0, tiled=True).reshape(128, D)
    routed = call(route_kernel, (128, D), spread)
    own = lax.all_to_all(routed.reshape(Z, 8, D), "z", 0, 0, tiled=True).reshape(128, D)
    left = shift(own, "x", 1)
    right = shift(own, "x", -1)
    far_low = shift(left[:64], "x", 1)
    far_high = shift(right[64:], "x", -1)
    place = jnp.stack([lax.axis_index("x"), lax.axis_index("c")]).astype(jnp.int32)
    pairs = [part for mine in (own, left, right) for part in (mine, shift(mine, "c", 1))]
    near = call(near_kernel, (768, 256), place, *pairs, weights, flops=6 * 10**9)
    far = call(stack_kernel, (128, D), far_low, far_high, near, far=(2,))
    mixed = call(far_kernel, (64, 16, 256), place, near, far, shift(far, "c", 1), weights, flops=2 * 10**9)
    mixed = lax.all_to_all(mixed, ("z", "y"), 0, 0, tiled=True)
    return call(place_kernel, (4, 256, 256), place, mixed)


def solution(mesh):
    grid = Mesh(mesh.devices.reshape(Z, Y, X, C), ("z", "y", "x", "c"))
    rows, columns = ("z", "y"), ("x", "c")
    return jax.shard_map(
        shards, mesh=grid, in_specs=(P(rows, columns, None), P(), P(rows, None, columns)),
        out_specs=P(rows, None, columns), check_vma=False,
    )
```

```python
import jax
import jax.numpy as jnp
from jax import lax
from jax.experimental import pallas as pl
from jax.experimental.pallas import tpu as pltpu
from jax.sharding import Mesh, PartitionSpec as P

BF, F32 = jnp.bfloat16, jnp.float32
Z, Y, X, C = 16, 4, 4, 2
D, HEAD = 4096, 128
VMEM = pltpu.VMEM


def iota(shape, dim):
    return lax.broadcasted_iota(jnp.int32, shape, dim)


def one_hot(source, n, m):
    return jnp.where(source(iota((n, m), 0)) == iota((n, m), 1), 1.0, 0.0).astype(BF)


def pick(matrix, rows):
    return jnp.dot(matrix, rows, preferred_element_type=F32).astype(BF)


def normalize_kernel(frames_ref, gain_ref, out_ref):
    rows = frames_ref[...].reshape(128, D).astype(F32)
    scale = lax.rsqrt(jnp.mean(rows * rows, axis=-1, keepdims=True) + 1e-05)
    shuffle = one_hot(lambda i: (((i >> 4) & 1) * 2 + (i & 1)) * 32 + (i >> 5) * 8 + ((i >> 1) & 7), 128, 128)
    for j in range(8):
        cut = slice(512 * j, 512 * (j + 1))
        out_ref[:, cut] = pick(shuffle, (rows[:, cut] * scale * gain_ref[:, cut]).astype(BF))


def route_kernel(in_ref, out_ref):
    order = one_hot(lambda i: ((i >> 1) & 3) * 32 + (i >> 3) * 2 + (i & 1), 128, 128)
    for j in range(8):
        cut = slice(512 * j, 512 * (j + 1))
        out_ref[:, cut] = pick(order, in_ref[:, cut])


def hold_kernel(*refs):
    pass


def project(token_refs, weights_ref):
    totals = [None] * 3
    for k in range(4):
        cut = slice(1024 * k, 1024 * (k + 1))
        part = jnp.concatenate([ref[:, cut] for ref in token_refs], axis=0)
        for c in range(3):
            weights = weights_ref[4 * k : 4 * (k + 1), :, c].reshape(1024, 256)
            term = jnp.dot(part, weights, preferred_element_type=F32)
            totals[c] = term if totals[c] is None else totals[c] + term
    return [total.astype(BF) for total in totals]


def attend(qkv, patches, core):
    def frame(i):
        return ((i & 127) >> 1) * 4 + ((i >> 7) ^ core) * 2 + (i & 1)

    keep = frame(iota((256, 256), 1)) <= frame(iota((256, 256), 0))
    scale = HEAD**-0.5 * 1.4426950408889634
    across = (((1,), (1,)), ((), ()))
    mixed = []
    for p in range(patches):
        units = [[part[256 * p : 256 * (p + 1), HEAD * h : HEAD * (h + 1)] for part in qkv] for h in range(2)]
        scores = [lax.dot_general(q, k, across, preferred_element_type=F32) * scale for q, k, _ in units]
        scores = [jnp.where(keep, s, -jnp.inf) for s in scores]
        grown = [jnp.exp2(s - jnp.max(s, axis=-1, keepdims=True)) for s in scores]
        probs = [(g * (1.0 / jnp.sum(g, axis=-1, keepdims=True))).astype(BF) for g in grown]
        heads = [jnp.dot(w, v, preferred_element_type=F32).astype(BF) for w, (_, _, v) in zip(probs, units)]
        mixed.append(jnp.concatenate(heads, axis=1))
    return mixed


def near_kernel(place_ref, *refs):
    *token_refs, weights_ref, out_ref = refs
    for p, mixed in enumerate(attend(project(token_refs, weights_ref), len(token_refs) // 2, place_ref[1])):
        out_ref[256 * p : 256 * (p + 1)] = mixed


def far_kernel(place_ref, first_ref, near_ref, far_ref, other_far_ref, weights_ref, out_ref):
    core = place_ref[1]
    (far,) = attend(project((far_ref, other_far_ref), weights_ref), 1, core)
    def source(i):
        return ((i >> 2) & 3) * 64 + (((i >> 1) & 1) ^ core) * 32 + (i >> 4) * 2 + (i & 1)

    order = one_hot(source, 256, 256)
    for k in range(4):
        cuts = [
            part[128 * g + 32 * k : 128 * g + 32 * (k + 1)]
            for part, halves in ((first_ref, 2), (near_ref, 4), (far, 2)) for g in range(halves)
        ]
        out_ref[16 * k : 16 * (k + 1)] = pick(order, jnp.concatenate(cuts, axis=0)).reshape(16, 16, 256)


def place_kernel(place_ref, mixed_ref, out_ref):
    def source(i):
        ahead = (((i >> 4) & 3) - place_ref[0]) & 3
        slot = jnp.where((ahead & 1) == 0, ahead + (ahead >> 1), jnp.where(ahead == 3 - 2 * place_ref[1], 1, 2))
        return (i & 7) * 32 + ((i >> 3) & 1) * 16 + slot * 4 + (i >> 6)

    order = one_hot(source, 256, 256)
    mixed = mixed_ref[...].reshape(2, 8, 2, 32, 256)
    for core in range(C):
        for pair in range(2):
            rows = pick(order, mixed[core, :, pair].reshape(256, 256))
            for f in range(4):
                for x in range(X):
                    start = 64 * x + 32 * core + 16 * pair
                    out_ref[f, start : start + 16] = rows[64 * f + 16 * x : 64 * f + 16 * (x + 1)]


def call(kernel, out_shape, *operands, flops=10**7, far=(), in_place=False):
    def spec(i, operand):
        return pl.BlockSpec(memory_space=pltpu.SMEM if operand.dtype == jnp.int32 else pl.ANY if i in far or in_place else VMEM)

    shapes = out_shape if isinstance(out_shape, list) else [out_shape]
    outs = pl.pallas_call(
        kernel,
        out_shape=[jax.ShapeDtypeStruct(shape, BF) for shape in shapes],
        in_specs=[spec(i, operand) for i, operand in enumerate(operands)],
        out_specs=[pl.BlockSpec(memory_space=pl.ANY if in_place else VMEM)] * len(shapes),
        input_output_aliases={i: i for i in range(len(shapes))} if in_place else {},
        compiler_params=pltpu.CompilerParams(vmem_limit_bytes=40 * 2**20),
        cost_estimate=pl.CostEstimate(flops=flops, bytes_accessed=2**21, transcendentals=0),
    )(*operands)
    return outs if isinstance(out_shape, list) else outs[0]


def send(rows, to):
    pairs = []
    for x in range(X):
        for c in range(C):
            there, core = to(x, c)
            pairs.append((x * C + c, there % X * C + core))
    return lax.ppermute(rows, ("x", "c"), pairs)


def shards(frames, norm_gain, w_qkv):
    weights = jnp.broadcast_to(jnp.transpose(w_qkv, (1, 0, 2)), (Y, 3, 64, 256))
    weights = lax.all_to_all(weights, "y", 0, 0, tiled=True)
    weights = lax.all_gather(weights, "z", axis=0)
    packed = call(normalize_kernel, (128, D), frames, norm_gain.reshape(1, D))
    spread = lax.all_to_all(packed.reshape(8, 16, D), ("y", "c"), 0, 0, tiled=True).reshape(128, D)
    routed = call(route_kernel, (128, D), spread)
    own = lax.all_to_all(routed.reshape(Z, 8, D), "z", 0, 0, tiled=True).reshape(128, D)
    place = jnp.stack([lax.axis_index("x"), lax.axis_index("c")]).astype(jnp.int32)
    straight = send(own, lambda x, c: (x + 1 - 2 * c, c))
    crossed = send(own, lambda x, c: (x - 1 + 2 * c, 1 - c))
    far = send(straight, lambda x, c: (x + 1 - 2 * c, c))
    swap = lambda rows: send(rows, lambda x, c: (x, 1 - c))
    held = call(hold_kernel, [crossed.shape], crossed, flops=10**10, in_place=True)[0]
    first = call(near_kernel, (256, 256), place, own, swap(own), weights, flops=2 * 10**9)
    near = call(near_kernel, (512, 256), place, straight, held, swap(held), swap(straight), weights, flops=4 * 10**9)
    far = call(hold_kernel, [far.shape], far, first, in_place=True)[0]
    mixed = call(far_kernel, (64, 16, 256), place, first, near, far, swap(far), weights, flops=2 * 10**9)
    mixed = lax.all_to_all(mixed, ("z", "y"), 0, 0, tiled=True)
    return call(place_kernel, (4, 256, 256), place, mixed)


def solution(mesh):
    grid = Mesh(mesh.devices.reshape(Z, Y, X, C), ("z", "y", "x", "c"))
    rows, columns = ("z", "y"), ("x", "c")
    return jax.shard_map(
        shards, mesh=grid, in_specs=(P(rows, columns, None), P(), P(rows, None, columns)),
        out_specs=P(rows, None, columns), check_vma=False,
    )
```

```python
import jax
import jax.numpy as jnp
from jax import lax
from jax.experimental import pallas as pl
from jax.experimental.pallas import tpu as pltpu
from jax.sharding import Mesh, PartitionSpec as P

BF, F32 = jnp.bfloat16, jnp.float32
Z, Y, X, C = 16, 4, 4, 2
D, HEAD = 4096, 128
VMEM = pltpu.VMEM


def iota(shape, dim):
    return lax.broadcasted_iota(jnp.int32, shape, dim)


def one_hot(source, n, m):
    return jnp.where(source(iota((n, m), 0)) == iota((n, m), 1), 1.0, 0.0).astype(BF)


def pick(matrix, rows):
    return jnp.dot(matrix, rows, preferred_element_type=F32).astype(BF)


def normalize_kernel(frames_ref, gain_ref, out_ref):
    rows = frames_ref[...].reshape(128, D).astype(F32)
    scale = lax.rsqrt(jnp.mean(rows * rows, axis=-1, keepdims=True) + 1e-05)
    shuffle = one_hot(
        lambda i: (i & 3) * 128 + ((i >> 3) & 1) * 64 + ((i >> 2) & 1) * 32 + (i >> 4), 512, 512
    )
    for j in range(2):
        cuts = [slice(1024 * q + 512 * j, 1024 * q + 512 * (j + 1)) for q in range(4)]
        normed = jnp.concatenate([(rows[:, cut] * scale * gain_ref[:, cut]).astype(BF) for cut in cuts], axis=0)
        out_ref[:, 512 * j : 512 * (j + 1)] = pick(shuffle, normed)


def merge_kernel(in_ref, out_ref):
    for q in range(4):
        order = one_hot(lambda i: i * 4 + q, 128, 512)
        for j in range(2):
            start = 1024 * q + 512 * j
            out_ref[:, start : start + 512] = pick(order, in_ref[:, 512 * j : 512 * (j + 1)])


def hold_kernel(*refs):
    pass


def project(token_refs, weights_ref, held_ref, arrived):
    parts = [pl.ds(4 * k, 4) for k in range(4)]
    copies = [pltpu.make_async_copy(weights_ref.at[part], held_ref.at[part], arrived.at[k]) for k, part in enumerate(parts)]
    for copy in copies:
        copy.start()
    totals = [None] * 3
    for k, copy in enumerate(copies):
        cut = slice(1024 * k, 1024 * (k + 1))
        rows = jnp.concatenate([ref[:, cut] for ref in token_refs], axis=0)
        copy.wait()
        for c in range(3):
            weights = held_ref[4 * k : 4 * (k + 1), :, c].reshape(1024, 256)
            term = jnp.dot(rows, weights, preferred_element_type=F32)
            totals[c] = term if totals[c] is None else totals[c] + term
    return [total.astype(BF) for total in totals]


def attend(qkv, patches, core):
    def frame(i):
        return ((i & 127) >> 1) * 4 + ((i >> 7) ^ core) * 2 + (i & 1)

    keep = frame(iota((256, 256), 1)) <= frame(iota((256, 256), 0))
    scale = HEAD**-0.5 * 1.4426950408889634
    across = (((1,), (1,)), ((), ()))
    units = [
        [part[256 * p : 256 * (p + 1), HEAD * h : HEAD * (h + 1)] for part in qkv] for p in range(patches) for h in range(2)
    ]
    scores = [lax.dot_general(q, k, across, preferred_element_type=F32) * scale for q, k, _ in units]
    scores = [jnp.where(keep, s, -jnp.inf) for s in scores]
    grown = [jnp.exp2(s - jnp.max(s, axis=-1, keepdims=True)) for s in scores]
    probs = [(g * (1.0 / jnp.sum(g, axis=-1, keepdims=True))).astype(BF) for g in grown]
    heads = [jnp.dot(w, v, preferred_element_type=F32).astype(BF) for w, (_, _, v) in zip(probs, units)]
    return [jnp.concatenate(heads[2 * p : 2 * p + 2], axis=1) for p in range(patches)]


def patches_kernel(place_ref, *refs):
    *token_refs, weights_ref, out_ref, held_ref, arrived = refs
    core = place_ref[1]
    mixed = attend(project(token_refs, weights_ref, held_ref, arrived), 4, core)
    def source(i):
        return ((i >> 2) & 3) * 64 + (((i >> 1) & 1) ^ core) * 32 + (i >> 4) * 2 + (i & 1)

    order = one_hot(source, 256, 256)
    for k in range(4):
        cuts = [part[128 * g + 32 * k : 128 * g + 32 * (k + 1)] for part in mixed for g in range(2)]
        out_ref[16 * k : 16 * (k + 1)] = pick(order, jnp.concatenate(cuts, axis=0)).reshape(16, 16, 256)


def place_kernel(place_ref, mixed_ref, out_ref):
    def source(i):
        ahead = (((i >> 4) & 3) - place_ref[0]) & 3
        slot = jnp.where((ahead & 1) == 0, ahead + (ahead >> 1), jnp.where(ahead == 3 - 2 * place_ref[1], 1, 2))
        return ((i >> 1) & 7) * 32 + (i & 1) * 16 + slot * 4 + (i >> 6)

    order = one_hot(source, 256, 256)
    mixed = mixed_ref[...].reshape(2, 8, 2, 2, 16, 256)
    for core in range(C):
        for upper in range(2):
            rows = pick(order, mixed[upper, :, :, core].reshape(256, 256))
            for f in range(4):
                for x in range(X):
                    start = 64 * x + 32 * core + 16 * upper
                    out_ref[f, start : start + 16] = rows[64 * f + 16 * x : 64 * f + 16 * (x + 1)]


def call(kernel, out_shape, *operands, flops=10**7, far=(), in_place=False, scratch=(), limit=40):
    def spec(i, operand):
        return pl.BlockSpec(memory_space=pltpu.SMEM if operand.dtype == jnp.int32 else pl.ANY if i in far or in_place else VMEM)

    shapes = out_shape if isinstance(out_shape, list) else [out_shape]
    outs = pl.pallas_call(
        kernel,
        out_shape=[jax.ShapeDtypeStruct(shape, BF) for shape in shapes],
        in_specs=[spec(i, operand) for i, operand in enumerate(operands)],
        out_specs=[pl.BlockSpec(memory_space=pl.ANY if in_place else VMEM)] * len(shapes),
        input_output_aliases={i: i for i in range(len(shapes))} if in_place else {},
        scratch_shapes=scratch,
        compiler_params=pltpu.CompilerParams(vmem_limit_bytes=limit * 2**20),
        cost_estimate=pl.CostEstimate(flops=flops, bytes_accessed=2**21, transcendentals=0),
    )(*operands)
    return outs if isinstance(out_shape, list) else outs[0]


def send(rows, to):
    pairs = []
    for x in range(X):
        for c in range(C):
            there, core = to(x, c)
            pairs.append((x * C + c, there % X * C + core))
    return lax.ppermute(rows, ("x", "c"), pairs)


def send_home(rows, to):
    pairs = []
    for y in range(Y):
        for x in range(X):
            for c in range(C):
                there, core = to(x, c)
                held = ((y - y % 2 + c) * X + x) * C + y % 2
                pairs.append((held, (y * X + there % X) * C + core))
    return lax.ppermute(rows, ("y", "x", "c"), pairs)


def shards(frames, norm_gain, w_qkv):
    weights = jnp.broadcast_to(jnp.transpose(w_qkv, (1, 0, 2)), (Y, 3, 64, 256))
    weights = lax.all_to_all(weights, "y", 0, 0, tiled=True)
    weights = lax.all_gather(weights, "z", axis=0)
    packed = call(normalize_kernel, (512, 1024), frames, norm_gain.reshape(1, D))
    spread = lax.all_to_all(packed.reshape(64, 8, 1024), ("z", "y"), 0, 0, tiled=True)
    rows = call(merge_kernel, (128, D), spread.reshape(512, 1024))
    place = jnp.stack([lax.axis_index("x"), lax.axis_index("c")]).astype(jnp.int32)
    straight = send_home(rows, lambda x, c: (x + 1 - 2 * c, c))
    crossed = send_home(rows, lambda x, c: (x - 1 + 2 * c, 1 - c))
    own = send_home(rows, lambda x, c: (x, c))
    far = send(straight, lambda x, c: (x + 1 - 2 * c, c))
    swap = lambda part: send(part, lambda x, c: (x, 1 - c))
    held = call(hold_kernel, [crossed.shape], crossed, flops=10**10, in_place=True)[0]
    tokens = (own, swap(own), straight, held, swap(held), swap(straight), far, swap(far))
    mixed = call(
        patches_kernel, (64, 16, 256), place, *tokens, weights, flops=8 * 10**9, far=(9,), limit=44,
        scratch=(VMEM((Z, Y, 3, 64, 256), BF), pltpu.SemaphoreType.DMA((4,))),
    )
    mixed = lax.all_to_all(mixed, ("z", "y"), 0, 0, tiled=True)
    return call(place_kernel, (4, 256, 256), place, mixed)


def solution(mesh):
    grid = Mesh(mesh.devices.reshape(Z, Y, X, C), ("z", "y", "x", "c"))
    rows, columns = ("z", "y"), ("x", "c")
    return jax.shard_map(
        shards, mesh=grid, in_specs=(P(rows, columns, None), P(), P(rows, None, columns)),
        out_specs=P(rows, None, columns), check_vma=False,
    )
```

```python
import jax
import jax.numpy as jnp
from jax import lax
from jax.experimental import pallas as pl
from jax.experimental.pallas import tpu as pltpu
from jax.sharding import Mesh, PartitionSpec as P

BF, F32 = jnp.bfloat16, jnp.float32
Z, Y, X, C = 16, 4, 4, 2
D, HEAD = 4096, 128
VMEM = pltpu.VMEM


def iota(shape, dim):
    return lax.broadcasted_iota(jnp.int32, shape, dim)


def one_hot(source, n, m):
    return jnp.where(source(iota((n, m), 0)) == iota((n, m), 1), 1.0, 0.0).astype(BF)


def pick(matrix, rows):
    return jnp.dot(matrix, rows, preferred_element_type=F32).astype(BF)


def normalize_kernel(frames_ref, gain_ref, out_ref):
    rows = frames_ref[...].reshape(128, D).astype(F32)
    scale = lax.rsqrt(jnp.mean(rows * rows, axis=-1, keepdims=True) + 1e-05)
    shuffle = one_hot(
        lambda i: (i & 3) * 128 + ((i >> 3) & 1) * 64 + ((i >> 2) & 1) * 32 + (i >> 4), 512, 512
    )
    for j in range(2):
        cuts = [slice(1024 * q + 512 * j, 1024 * q + 512 * (j + 1)) for q in range(4)]
        normed = jnp.concatenate([(rows[:, cut] * scale * gain_ref[:, cut]).astype(BF) for cut in cuts], axis=0)
        out_ref[:, 512 * j : 512 * (j + 1)] = pick(shuffle, normed)


def merge_kernel(in_ref, out_ref):
    for q in range(4):
        order = one_hot(lambda i: i * 4 + q, 128, 512)
        for j in range(2):
            start = 1024 * q + 512 * j
            out_ref[:, start : start + 512] = pick(order, in_ref[:, 512 * j : 512 * (j + 1)])


def hold_kernel(*refs):
    pass


def project(token_refs, weights_ref, rows_ref, held_ref, arrived):
    n = len(token_refs)
    arrivals = []
    for k in range(4):
        part, cut = pl.ds(4 * k, 4), pl.ds(1024 * k, 1024)
        copies = [
            pltpu.make_async_copy(ref.at[:, cut], rows_ref.at[pl.ds(128 * p, 128), cut], arrived.at[k, p])
            for p, ref in enumerate(token_refs)
        ]
        copies.append(pltpu.make_async_copy(weights_ref.at[part], held_ref.at[part], arrived.at[k, n]))
        for copy in copies:
            copy.start()
        arrivals.append(copies)
    totals = [None] * 3
    for k, copies in enumerate(arrivals):
        for copy in copies:
            copy.wait()
        rows = rows_ref[:, 1024 * k : 1024 * (k + 1)]
        for c in range(3):
            weights = held_ref[4 * k : 4 * (k + 1), :, c].reshape(1024, 256)
            term = jnp.dot(rows, weights, preferred_element_type=F32)
            totals[c] = term if totals[c] is None else totals[c] + term
    return [total.astype(BF) for total in totals]


def attend(qkv, patches, core):
    def frame(i):
        return ((i & 127) >> 1) * 4 + ((i >> 7) ^ core) * 2 + (i & 1)

    keep = frame(iota((256, 256), 1)) <= frame(iota((256, 256), 0))
    scale = HEAD**-0.5 * 1.4426950408889634
    across = (((1,), (1,)), ((), ()))
    units = [
        [part[256 * p : 256 * (p + 1), HEAD * h : HEAD * (h + 1)] for part in qkv] for p in range(patches) for h in range(2)
    ]
    scores = [lax.dot_general(q, k, across, preferred_element_type=F32) * scale for q, k, _ in units]
    scores = [jnp.where(keep, s, -jnp.inf) for s in scores]
    grown = [jnp.exp2(s - jnp.max(s, axis=-1, keepdims=True)) for s in scores]
    probs = [(g * (1.0 / jnp.sum(g, axis=-1, keepdims=True))).astype(BF) for g in grown]
    heads = [jnp.dot(w, v, preferred_element_type=F32).astype(BF) for w, (_, _, v) in zip(probs, units)]
    return [jnp.concatenate(heads[2 * p : 2 * p + 2], axis=1) for p in range(patches)]


def patches_kernel(place_ref, *refs):
    *token_refs, weights_ref, out_ref, rows_ref, held_ref, arrived = refs
    core = place_ref[1]
    mixed = attend(project(token_refs, weights_ref, rows_ref, held_ref, arrived), 4, core)
    def source(i):
        return ((i >> 2) & 3) * 64 + (((i >> 1) & 1) ^ core) * 32 + (i >> 4) * 2 + (i & 1)

    order = one_hot(source, 256, 256)
    for k in range(4):
        cuts = [part[128 * g + 32 * k : 128 * g + 32 * (k + 1)] for part in mixed for g in range(2)]
        out_ref[16 * k : 16 * (k + 1)] = pick(order, jnp.concatenate(cuts, axis=0)).reshape(16, 16, 256)


def place_kernel(place_ref, mixed_ref, out_ref):
    def source(i):
        ahead = (((i >> 4) & 3) - place_ref[0]) & 3
        slot = jnp.where((ahead & 1) == 0, ahead + (ahead >> 1), jnp.where(ahead == 3 - 2 * place_ref[1], 1, 2))
        return ((i >> 1) & 7) * 32 + (i & 1) * 16 + slot * 4 + (i >> 6)

    order = one_hot(source, 256, 256)
    mixed = mixed_ref[...].reshape(2, 8, 2, 2, 16, 256)
    for core in range(C):
        for upper in range(2):
            rows = pick(order, mixed[upper, :, :, core].reshape(256, 256))
            for f in range(4):
                for x in range(X):
                    start = 64 * x + 32 * core + 16 * upper
                    out_ref[f, start : start + 16] = rows[64 * f + 16 * x : 64 * f + 16 * (x + 1)]


def call(kernel, out_shape, *operands, flops=10**7, far=(), in_place=False, scratch=(), limit=40):
    def spec(i, operand):
        return pl.BlockSpec(memory_space=pltpu.SMEM if operand.dtype == jnp.int32 else pl.ANY if i in far or in_place else VMEM)

    shapes = out_shape if isinstance(out_shape, list) else [out_shape]
    outs = pl.pallas_call(
        kernel,
        out_shape=[jax.ShapeDtypeStruct(shape, BF) for shape in shapes],
        in_specs=[spec(i, operand) for i, operand in enumerate(operands)],
        out_specs=[pl.BlockSpec(memory_space=pl.ANY if in_place else VMEM)] * len(shapes),
        input_output_aliases={i: i for i in range(len(shapes))} if in_place else {},
        scratch_shapes=scratch,
        compiler_params=pltpu.CompilerParams(vmem_limit_bytes=limit * 2**20),
        cost_estimate=pl.CostEstimate(flops=flops, bytes_accessed=2**21, transcendentals=0),
    )(*operands)
    return outs if isinstance(out_shape, list) else outs[0]


def send(rows, to):
    pairs = []
    for x in range(X):
        for c in range(C):
            there, core = to(x, c)
            pairs.append((x * C + c, there % X * C + core))
    return lax.ppermute(rows, ("x", "c"), pairs)


def send_home(rows, to):
    pairs = []
    for y in range(Y):
        for x in range(X):
            for c in range(C):
                there, core = to(x, c)
                held = ((y - y % 2 + c) * X + x) * C + y % 2
                pairs.append((held, (y * X + there % X) * C + core))
    return lax.ppermute(rows, ("y", "x", "c"), pairs)


def shards(frames, norm_gain, w_qkv):
    weights = jnp.broadcast_to(jnp.transpose(w_qkv, (1, 0, 2)), (Y, 3, 64, 256))
    weights = lax.all_to_all(weights, "y", 0, 0, tiled=True)
    weights = lax.all_gather(weights, "z", axis=0)
    packed = call(normalize_kernel, (512, 1024), frames, norm_gain.reshape(1, D))
    spread = lax.all_to_all(packed.reshape(64, 8, 1024), ("z", "y"), 0, 0, tiled=True)
    rows = call(merge_kernel, (128, D), spread.reshape(512, 1024))
    place = jnp.stack([lax.axis_index("x"), lax.axis_index("c")]).astype(jnp.int32)
    straight = send_home(rows, lambda x, c: (x + 1 - 2 * c, c))
    crossed = send_home(rows, lambda x, c: (x - 1 + 2 * c, 1 - c))
    own = send_home(rows, lambda x, c: (x, c))
    far = send(straight, lambda x, c: (x + 1 - 2 * c, c))
    swap = lambda part: send(part, lambda x, c: (x, 1 - c))
    held = call(hold_kernel, [crossed.shape], crossed, flops=10**10, in_place=True)[0]
    tokens = (own, swap(own), straight, held, swap(held), swap(straight), far, swap(far))
    mixed = call(
        patches_kernel, (64, 16, 256), place, *tokens, weights, flops=8 * 10**9, far=range(1, 10), limit=44,
        scratch=(VMEM((1024, D), BF), VMEM((Z, Y, 3, 64, 256), BF), pltpu.SemaphoreType.DMA((4, 9))),
    )
    mixed = lax.all_to_all(mixed, ("z", "y"), 0, 0, tiled=True)
    return call(place_kernel, (4, 256, 256), place, mixed)


def solution(mesh):
    grid = Mesh(mesh.devices.reshape(Z, Y, X, C), ("z", "y", "x", "c"))
    rows, columns = ("z", "y"), ("x", "c")
    return jax.shard_map(
        shards, mesh=grid, in_specs=(P(rows, columns, None), P(), P(rows, None, columns)),
        out_specs=P(rows, None, columns), check_vma=False,
    )
```

```python
import jax
import jax.numpy as jnp
from jax import lax
from jax.experimental import pallas as pl
from jax.experimental.pallas import tpu as pltpu
from jax.sharding import Mesh, PartitionSpec as P

BF, F32 = jnp.bfloat16, jnp.float32
Z, Y, X, C = 16, 4, 4, 2
D, HEAD = 4096, 128
VMEM = pltpu.VMEM


def iota(shape, dim):
    return lax.broadcasted_iota(jnp.int32, shape, dim)


def one_hot(source, n, m):
    return jnp.where(source(iota((n, m), 0)) == iota((n, m), 1), 1.0, 0.0).astype(BF)


def pick(matrix, rows):
    return jnp.dot(matrix, rows, preferred_element_type=F32).astype(BF)


def normalize_kernel(frames_ref, gain_ref, out_ref):
    rows = frames_ref[...].reshape(128, D).astype(F32)
    scale = lax.rsqrt(jnp.mean(rows * rows, axis=-1, keepdims=True) + 1e-05)
    shuffle = one_hot(
        lambda i: (i & 3) * 128 + ((i >> 3) & 1) * 64 + ((i >> 2) & 1) * 32 + (i >> 4), 512, 512
    )
    for j in range(2):
        cuts = [slice(1024 * q + 512 * j, 1024 * q + 512 * (j + 1)) for q in range(4)]
        normed = jnp.concatenate([(rows[:, cut] * scale * gain_ref[:, cut]).astype(BF) for cut in cuts], axis=0)
        out_ref[:, 512 * j : 512 * (j + 1)] = pick(shuffle, normed)


def merge_kernel(in_ref, out_ref):
    for q in range(4):
        order = one_hot(lambda i: i * 4 + q, 128, 512)
        for j in range(2):
            start = 1024 * q + 512 * j
            out_ref[:, start : start + 512] = pick(order, in_ref[:, 512 * j : 512 * (j + 1)])


def hold_kernel(*refs):
    pass


def project(token_refs, weights_ref, rows_ref, held_ref, arrived):
    n = len(token_refs)
    arrivals = []
    for k in range(4):
        part, cut = pl.ds(4 * k, 4), pl.ds(1024 * k, 1024)
        copies = [
            pltpu.make_async_copy(ref.at[:, cut], rows_ref.at[pl.ds(128 * p, 128), cut], arrived.at[k, p])
            for p, ref in enumerate(token_refs)
        ]
        copies.append(pltpu.make_async_copy(weights_ref.at[part], held_ref.at[part], arrived.at[k, n]))
        for copy in copies:
            copy.start()
        arrivals.append(copies)
    totals = [None] * 3
    for k, copies in enumerate(arrivals):
        for copy in copies:
            copy.wait()
        rows = rows_ref[:, 1024 * k : 1024 * (k + 1)]
        for c in range(3):
            weights = held_ref[4 * k : 4 * (k + 1), :, c].reshape(1024, 256)
            term = jnp.dot(rows, weights, preferred_element_type=F32)
            totals[c] = term if totals[c] is None else totals[c] + term
    return [total.astype(BF) for total in totals]


def attend(qkv, patches, core):
    def frame(i):
        return ((i & 127) >> 1) * 4 + ((i >> 7) ^ core) * 2 + (i & 1)

    keep = frame(iota((256, 256), 1)) <= frame(iota((256, 256), 0))
    scale = HEAD**-0.5 * 1.4426950408889634
    across = (((1,), (1,)), ((), ()))
    units = [
        [part[256 * p : 256 * (p + 1), HEAD * h : HEAD * (h + 1)] for part in qkv] for p in range(patches) for h in range(2)
    ]
    scores = [lax.dot_general(q, k, across, preferred_element_type=F32) * scale for q, k, _ in units]
    scores = [jnp.where(keep, s, -jnp.inf) for s in scores]
    grown = [jnp.exp2(s - jnp.max(s, axis=-1, keepdims=True)) for s in scores]
    probs = [(g * (1.0 / jnp.sum(g, axis=-1, keepdims=True))).astype(BF) for g in grown]
    heads = [jnp.dot(w, v, preferred_element_type=F32).astype(BF) for w, (_, _, v) in zip(probs, units)]
    return [jnp.concatenate(heads[2 * p : 2 * p + 2], axis=1) for p in range(patches)]


def patches_kernel(place_ref, *refs):
    *token_refs, weights_ref, out_ref, rows_ref, held_ref, arrived = refs
    core = place_ref[1]
    mixed = attend(project(token_refs, weights_ref, rows_ref, held_ref, arrived), 4, core)
    def source(i):
        return ((i >> 2) & 3) * 64 + (((i >> 1) & 1) ^ core) * 32 + (i >> 4) * 2 + (i & 1)

    order = one_hot(source, 256, 256)
    for k in range(4):
        cuts = [part[128 * g + 32 * k : 128 * g + 32 * (k + 1)] for part in mixed for g in range(2)]
        out_ref[16 * k : 16 * (k + 1)] = pick(order, jnp.concatenate(cuts, axis=0)).reshape(16, 16, 256)


def place_kernel(place_ref, mixed_ref, out_ref):
    def source(i):
        ahead = (((i >> 4) & 3) - place_ref[0]) & 3
        slot = jnp.where((ahead & 1) == 0, ahead + (ahead >> 1), jnp.where(ahead == 3 - 2 * place_ref[1], 1, 2))
        return ((i >> 1) & 7) * 32 + (i & 1) * 16 + slot * 4 + (i >> 6)

    order = one_hot(source, 256, 256)
    mixed = mixed_ref[...].reshape(2, 8, 2, 2, 16, 256)
    for core in range(C):
        for upper in range(2):
            rows = pick(order, mixed[upper, :, :, core].reshape(256, 256))
            for f in range(4):
                for x in range(X):
                    start = 64 * x + 32 * core + 16 * upper
                    out_ref[f, start : start + 16] = rows[64 * f + 16 * x : 64 * f + 16 * (x + 1)]


def call(kernel, out_shape, *operands, flops=10**7, far=(), in_place=False, scratch=(), limit=40):
    def spec(i, operand):
        return pl.BlockSpec(memory_space=pltpu.SMEM if operand.dtype == jnp.int32 else pl.ANY if i in far or in_place else VMEM)

    shapes = out_shape if isinstance(out_shape, list) else [out_shape]
    outs = pl.pallas_call(
        kernel,
        out_shape=[jax.ShapeDtypeStruct(shape, BF) for shape in shapes],
        in_specs=[spec(i, operand) for i, operand in enumerate(operands)],
        out_specs=[pl.BlockSpec(memory_space=pl.ANY if in_place else VMEM)] * len(shapes),
        input_output_aliases={i: i for i in range(len(shapes))} if in_place else {},
        scratch_shapes=scratch,
        compiler_params=pltpu.CompilerParams(vmem_limit_bytes=limit * 2**20),
        cost_estimate=pl.CostEstimate(flops=flops, bytes_accessed=2**21, transcendentals=0),
    )(*operands)
    return outs if isinstance(out_shape, list) else outs[0]


def send(rows, to):
    pairs = []
    for x in range(X):
        for c in range(C):
            there, core = to(x, c)
            pairs.append((x * C + c, there % X * C + core))
    return lax.ppermute(rows, ("x", "c"), pairs)


def send_home(rows, to):
    pairs = []
    for y in range(Y):
        for x in range(X):
            for c in range(C):
                there, core = to(x, c)
                held = ((y - y % 2 + c) * X + x) * C + y % 2
                pairs.append((held, (y * X + there % X) * C + core))
    return lax.ppermute(rows, ("y", "x", "c"), pairs)


def shards(frames, norm_gain, w_qkv):
    weights = jnp.broadcast_to(jnp.transpose(w_qkv, (1, 0, 2)), (Y, 3, 64, 256))
    weights = lax.all_to_all(weights, "y", 0, 0, tiled=True)
    packed = call(normalize_kernel, (512, 1024), frames, norm_gain.reshape(1, D))
    weights = call(hold_kernel, [weights.shape], weights, packed, in_place=True)[0]
    weights = lax.all_gather(weights, "z", axis=0)
    spread = lax.all_to_all(packed.reshape(64, 8, 1024), ("z", "y"), 0, 0, tiled=True)
    rows = call(merge_kernel, (128, D), spread.reshape(512, 1024))
    place = jnp.stack([lax.axis_index("x"), lax.axis_index("c")]).astype(jnp.int32)
    straight = send_home(rows, lambda x, c: (x + 1 - 2 * c, c))
    crossed = send_home(rows, lambda x, c: (x - 1 + 2 * c, 1 - c))
    own = send_home(rows, lambda x, c: (x, c))
    far = send(straight, lambda x, c: (x + 1 - 2 * c, c))
    swap = lambda part: send(part, lambda x, c: (x, 1 - c))
    held = call(hold_kernel, [crossed.shape], crossed, flops=10**10, in_place=True)[0]
    tokens = (own, swap(own), straight, held, swap(held), swap(straight), far, swap(far))
    mixed = call(
        patches_kernel, (64, 16, 256), place, *tokens, weights, flops=8 * 10**9, far=range(1, 10), limit=44,
        scratch=(VMEM((1024, D), BF), VMEM((Z, Y, 3, 64, 256), BF), pltpu.SemaphoreType.DMA((4, 9))),
    )
    mixed = lax.all_to_all(mixed, ("z", "y"), 0, 0, tiled=True)
    return call(place_kernel, (4, 256, 256), place, mixed)


def solution(mesh):
    grid = Mesh(mesh.devices.reshape(Z, Y, X, C), ("z", "y", "x", "c"))
    rows, columns = ("z", "y"), ("x", "c")
    return jax.shard_map(
        shards, mesh=grid, in_specs=(P(rows, columns, None), P(), P(rows, None, columns)),
        out_specs=P(rows, None, columns), check_vma=False,
    )
```

```python
import jax
import jax.numpy as jnp
from jax import lax
from jax.experimental import pallas as pl
from jax.experimental.pallas import tpu as pltpu
from jax.sharding import Mesh, PartitionSpec as P

BF, F32 = jnp.bfloat16, jnp.float32
Z, Y, X, C = 16, 4, 4, 2
D, HEAD = 4096, 128
VMEM = pltpu.VMEM


def iota(shape, dim):
    return lax.broadcasted_iota(jnp.int32, shape, dim)


def one_hot(source, n, m):
    return jnp.where(source(iota((n, m), 0)) == iota((n, m), 1), 1.0, 0.0).astype(BF)


def pick(matrix, rows):
    return jnp.dot(matrix, rows, preferred_element_type=F32).astype(BF)


def normalize_kernel(frames_ref, gain_ref, out_ref):
    rows = frames_ref[...].reshape(128, D).astype(F32)
    scale = lax.rsqrt(jnp.mean(rows * rows, axis=-1, keepdims=True) + 1e-05)
    shuffle = one_hot(
        lambda i: (i & 3) * 128 + ((i >> 3) & 1) * 64 + ((i >> 2) & 1) * 32 + (i >> 4), 512, 512
    )
    for j in range(2):
        cuts = [slice(1024 * q + 512 * j, 1024 * q + 512 * (j + 1)) for q in range(4)]
        normed = jnp.concatenate([(rows[:, cut] * scale * gain_ref[:, cut]).astype(BF) for cut in cuts], axis=0)
        out_ref[:, 512 * j : 512 * (j + 1)] = pick(shuffle, normed)


def merge_kernel(in_ref, out_ref):
    for q in range(4):
        order = one_hot(lambda i: i * 4 + q, 128, 512)
        for j in range(2):
            start = 1024 * q + 512 * j
            out_ref[:, start : start + 512] = pick(order, in_ref[:, 512 * j : 512 * (j + 1)])


def hold_kernel(*refs):
    pass


def project(token_refs, weights_ref, rows_ref, held_ref, arrived):
    n = len(token_refs)
    arrivals = []
    for k in range(4):
        part, cut = pl.ds(4 * k, 4), pl.ds(1024 * k, 1024)
        copies = [
            pltpu.make_async_copy(ref.at[:, cut], rows_ref.at[pl.ds(128 * p, 128), cut], arrived.at[k, p])
            for p, ref in enumerate(token_refs)
        ]
        copies.append(pltpu.make_async_copy(weights_ref.at[part], held_ref.at[part], arrived.at[k, n]))
        for copy in copies:
            copy.start()
        arrivals.append(copies)
    totals = [None] * 3
    for k, copies in enumerate(arrivals):
        for copy in copies:
            copy.wait()
        rows = rows_ref[:, 1024 * k : 1024 * (k + 1)]
        for c in range(3):
            weights = held_ref[4 * k : 4 * (k + 1), :, c].reshape(1024, 256)
            term = jnp.dot(rows, weights, preferred_element_type=F32)
            totals[c] = term if totals[c] is None else totals[c] + term
    return [total.astype(BF) for total in totals]


def attend(qkv, patches, core):
    def frame(i):
        return ((i & 127) >> 1) * 4 + ((i >> 7) ^ core) * 2 + (i & 1)

    keep = frame(iota((256, 256), 1)) <= frame(iota((256, 256), 0))
    scale = HEAD**-0.5 * 1.4426950408889634
    across = (((1,), (1,)), ((), ()))
    units = [
        [part[256 * p : 256 * (p + 1), HEAD * h : HEAD * (h + 1)] for part in qkv] for p in range(patches) for h in range(2)
    ]
    scores = [lax.dot_general(q, k, across, preferred_element_type=F32) * scale for q, k, _ in units]
    scores = [jnp.where(keep, s, -jnp.inf) for s in scores]
    grown = [jnp.exp2(s - jnp.max(s, axis=-1, keepdims=True)) for s in scores]
    probs = [(g * (1.0 / jnp.sum(g, axis=-1, keepdims=True))).astype(BF) for g in grown]
    heads = [jnp.dot(w, v, preferred_element_type=F32).astype(BF) for w, (_, _, v) in zip(probs, units)]
    return [jnp.concatenate(heads[2 * p : 2 * p + 2], axis=1) for p in range(patches)]


def patches_kernel(place_ref, *refs):
    *token_refs, weights_ref, out_ref, rows_ref, held_ref, arrived = refs
    core = place_ref[1]
    mixed = attend(project(token_refs, weights_ref, rows_ref, held_ref, arrived), 4, core)
    def source(i):
        return ((i >> 2) & 3) * 64 + (((i >> 1) & 1) ^ core) * 32 + (i >> 4) * 2 + (i & 1)

    order = one_hot(source, 256, 256)
    for k in range(4):
        cuts = [part[128 * g + 32 * k : 128 * g + 32 * (k + 1)] for part in mixed for g in range(2)]
        out_ref[16 * k : 16 * (k + 1)] = pick(order, jnp.concatenate(cuts, axis=0)).reshape(16, 16, 256)


def place_kernel(place_ref, mixed_ref, out_ref):
    def source(i):
        ahead = (((i >> 4) & 3) - place_ref[0]) & 3
        slot = jnp.where((ahead & 1) == 0, ahead + (ahead >> 1), jnp.where(ahead == 3 - 2 * place_ref[1], 1, 2))
        return ((i >> 1) & 7) * 32 + (i & 1) * 16 + slot * 4 + (i >> 6)

    order = one_hot(source, 256, 256)
    mixed = mixed_ref[...].reshape(2, 8, 2, 2, 16, 256)
    for core in range(C):
        for upper in range(2):
            rows = pick(order, mixed[upper, :, :, core].reshape(256, 256))
            for f in range(4):
                for x in range(X):
                    start = 64 * x + 32 * core + 16 * upper
                    out_ref[f, start : start + 16] = rows[64 * f + 16 * x : 64 * f + 16 * (x + 1)]


def call(kernel, out_shape, *operands, flops=10**7, far=(), in_place=False, scratch=(), limit=40):
    def spec(i, operand):
        return pl.BlockSpec(memory_space=pltpu.SMEM if operand.dtype == jnp.int32 else pl.ANY if i in far or in_place else VMEM)

    shapes = out_shape if isinstance(out_shape, list) else [out_shape]
    outs = pl.pallas_call(
        kernel,
        out_shape=[jax.ShapeDtypeStruct(shape, BF) for shape in shapes],
        in_specs=[spec(i, operand) for i, operand in enumerate(operands)],
        out_specs=[pl.BlockSpec(memory_space=pl.ANY if in_place else VMEM)] * len(shapes),
        input_output_aliases={i: i for i in range(len(shapes))} if in_place else {},
        scratch_shapes=scratch,
        compiler_params=pltpu.CompilerParams(vmem_limit_bytes=limit * 2**20),
        cost_estimate=pl.CostEstimate(flops=flops, bytes_accessed=2**21, transcendentals=0),
    )(*operands)
    return outs if isinstance(out_shape, list) else outs[0]


def send(rows, to):
    pairs = []
    for x in range(X):
        for c in range(C):
            there, core = to(x, c)
            pairs.append((x * C + c, there % X * C + core))
    return lax.ppermute(rows, ("x", "c"), pairs)


def send_home(rows, to):
    pairs = []
    for y in range(Y):
        for x in range(X):
            for c in range(C):
                there, core = to(x, c)
                held = ((y - y % 2 + c) * X + x) * C + y % 2
                pairs.append((held, (y * X + there % X) * C + core))
    return lax.ppermute(rows, ("y", "x", "c"), pairs)


def shards(frames, norm_gain, w_qkv):
    weights = jnp.broadcast_to(jnp.transpose(w_qkv, (1, 0, 2)), (Y, 3, 64, 256))
    weights = lax.all_to_all(weights, "y", 0, 0, tiled=True)
    packed = call(normalize_kernel, (512, 1024), frames, norm_gain.reshape(1, D))
    weights = call(hold_kernel, [weights.shape], weights, packed, in_place=True)[0]
    weights = lax.all_gather(weights, "z", axis=0)
    spread = lax.all_to_all(packed.reshape(64, 8, 1024), ("z", "y"), 0, 0, tiled=True)
    rows = call(merge_kernel, (128, D), spread.reshape(512, 1024))
    place = jnp.stack([lax.axis_index("x"), lax.axis_index("c")]).astype(jnp.int32)
    straight = send_home(rows, lambda x, c: (x + 1 - 2 * c, c))
    crossed = send_home(rows, lambda x, c: (x - 1 + 2 * c, 1 - c))
    own = send_home(rows, lambda x, c: (x, c))
    far = send(crossed, lambda x, c: (x + 1 - 2 * c, c))
    swap = lambda part: send(part, lambda x, c: (x, 1 - c))
    held = call(hold_kernel, [straight.shape], straight, flops=10**10, in_place=True)[0]
    tokens = (own, swap(own), held, crossed, swap(crossed), swap(held), swap(far), far)
    mixed = call(
        patches_kernel, (64, 16, 256), place, *tokens, weights, flops=8 * 10**9, far=range(1, 10), limit=44,
        scratch=(VMEM((1024, D), BF), VMEM((Z, Y, 3, 64, 256), BF), pltpu.SemaphoreType.DMA((4, 9))),
    )
    mixed = lax.all_to_all(mixed, ("z", "y"), 0, 0, tiled=True)
    return call(place_kernel, (4, 256, 256), place, mixed)


def solution(mesh):
    grid = Mesh(mesh.devices.reshape(Z, Y, X, C), ("z", "y", "x", "c"))
    rows, columns = ("z", "y"), ("x", "c")
    return jax.shard_map(
        shards, mesh=grid, in_specs=(P(rows, columns, None), P(), P(rows, None, columns)),
        out_specs=P(rows, None, columns), check_vma=False,
    )
```

```python
import jax
import jax.numpy as jnp
from jax import lax
from jax.experimental import pallas as pl
from jax.experimental.pallas import tpu as pltpu
from jax.sharding import Mesh, PartitionSpec as P

BF, F32 = jnp.bfloat16, jnp.float32
Z, Y, X, C = 16, 4, 4, 2
D, HEAD = 4096, 128
VMEM = pltpu.VMEM


def iota(shape, dim):
    return lax.broadcasted_iota(jnp.int32, shape, dim)


def one_hot(source, n, m):
    return jnp.where(source(iota((n, m), 0)) == iota((n, m), 1), 1.0, 0.0).astype(BF)


def pick(matrix, rows):
    return jnp.dot(matrix, rows, preferred_element_type=F32).astype(BF)


def normalize_kernel(frames_ref, gain_ref, out_ref):
    rows = frames_ref[...].reshape(128, D).astype(F32)
    scale = lax.rsqrt(jnp.mean(rows * rows, axis=-1, keepdims=True) + 1e-05)
    shuffle = one_hot(
        lambda i: (i & 3) * 128 + ((i >> 7) & 1) * 64 + ((i >> 2) & 1) * 32 + ((i >> 3) & 15) * 2 + (i >> 8), 512, 512
    )
    for j in range(2):
        cuts = [slice(1024 * q + 512 * j, 1024 * q + 512 * (j + 1)) for q in range(4)]
        normed = jnp.concatenate([(rows[:, cut] * scale * gain_ref[:, cut]).astype(BF) for cut in cuts], axis=0)
        out_ref[:, 512 * j : 512 * (j + 1)] = pick(shuffle, normed)


def merge_kernel(in_ref, out_ref):
    for q in range(4):
        order = one_hot(lambda i: ((((i >> 1) & 3) * 16 + (i >> 3)) * 2 + (i & 1)) * 4 + q, 128, 512)
        for j in range(2):
            start = 1024 * q + 512 * j
            out_ref[:, start : start + 512] = pick(order, in_ref[:, 512 * j : 512 * (j + 1)])


def hold_kernel(*refs):
    pass


def project(token_refs, weights_ref, rows_ref, held_ref, arrived):
    n = len(token_refs)
    arrivals = []
    for k in range(4):
        part, cut = pl.ds(4 * k, 4), pl.ds(1024 * k, 1024)
        copies = [
            pltpu.make_async_copy(ref.at[:, cut], rows_ref.at[pl.ds(128 * p, 128), cut], arrived.at[k, p])
            for p, ref in enumerate(token_refs)
        ]
        copies.append(pltpu.make_async_copy(weights_ref.at[part], held_ref.at[part], arrived.at[k, n]))
        for copy in copies:
            copy.start()
        arrivals.append(copies)
    totals = [None] * 3
    for k, copies in enumerate(arrivals):
        for copy in copies:
            copy.wait()
        rows = rows_ref[:, 1024 * k : 1024 * (k + 1)]
        for c in range(3):
            weights = held_ref[4 * k : 4 * (k + 1), :, c].reshape(1024, 256)
            term = jnp.dot(rows, weights, preferred_element_type=F32)
            totals[c] = term if totals[c] is None else totals[c] + term
    return [total.astype(BF) for total in totals]


def attend(qkv, patches, core):
    def frame(i):
        return ((i & 127) >> 1) * 4 + ((i >> 7) ^ core) * 2 + (i & 1)

    keep = frame(iota((256, 256), 1)) <= frame(iota((256, 256), 0))
    scale = HEAD**-0.5 * 1.4426950408889634
    across = (((1,), (1,)), ((), ()))
    units = [
        [part[256 * p : 256 * (p + 1), HEAD * h : HEAD * (h + 1)] for part in qkv] for p in range(patches) for h in range(2)
    ]
    scores = [lax.dot_general(q, k, across, preferred_element_type=F32) * scale for q, k, _ in units]
    scores = [jnp.where(keep, s, -jnp.inf) for s in scores]
    grown = [jnp.exp2(s - jnp.max(s, axis=-1, keepdims=True)) for s in scores]
    probs = [(g * (1.0 / jnp.sum(g, axis=-1, keepdims=True))).astype(BF) for g in grown]
    heads = [jnp.dot(w, v, preferred_element_type=F32).astype(BF) for w, (_, _, v) in zip(probs, units)]
    return [jnp.concatenate(heads[2 * p : 2 * p + 2], axis=1) for p in range(patches)]


def patches_kernel(place_ref, *refs):
    *token_refs, weights_ref, out_ref, rows_ref, held_ref, arrived = refs
    core = place_ref[1]
    mixed = attend(project(token_refs, weights_ref, rows_ref, held_ref, arrived), 4, core)
    def source(i):
        return ((i >> 2) & 3) * 64 + (((i >> 1) & 1) ^ core) * 32 + (i >> 4) * 2 + (i & 1)

    order = one_hot(source, 256, 256)
    for k in range(4):
        cuts = [part[128 * g + 32 * k : 128 * g + 32 * (k + 1)] for part in mixed for g in range(2)]
        out_ref[16 * k : 16 * (k + 1)] = pick(order, jnp.concatenate(cuts, axis=0)).reshape(16, 16, 256)


def place_kernel(place_ref, mixed_ref, out_ref):
    def source(i):
        ahead = (((i >> 4) & 3) - place_ref[0]) & 3
        slot = jnp.where((ahead & 1) == 0, ahead + (ahead >> 1), jnp.where(ahead == 3 - 2 * place_ref[1], 1, 2))
        return ((i >> 1) & 7) * 32 + (i & 1) * 16 + slot * 4 + (i >> 6)

    order = one_hot(source, 256, 256)
    mixed = mixed_ref[...].reshape(2, 8, 2, 2, 16, 256)
    for core in range(C):
        for upper in range(2):
            rows = pick(order, mixed[upper, :, :, core].reshape(256, 256))
            for f in range(4):
                for x in range(X):
                    start = 64 * x + 32 * core + 16 * upper
                    out_ref[f, start : start + 16] = rows[64 * f + 16 * x : 64 * f + 16 * (x + 1)]


def call(kernel, out_shape, *operands, flops=10**7, far=(), in_place=False, scratch=(), limit=40):
    def spec(i, operand):
        return pl.BlockSpec(memory_space=pltpu.SMEM if operand.dtype == jnp.int32 else pl.ANY if i in far or in_place else VMEM)

    shapes = out_shape if isinstance(out_shape, list) else [out_shape]
    outs = pl.pallas_call(
        kernel,
        out_shape=[jax.ShapeDtypeStruct(shape, BF) for shape in shapes],
        in_specs=[spec(i, operand) for i, operand in enumerate(operands)],
        out_specs=[pl.BlockSpec(memory_space=pl.ANY if in_place else VMEM)] * len(shapes),
        input_output_aliases={i: i for i in range(len(shapes))} if in_place else {},
        scratch_shapes=scratch,
        compiler_params=pltpu.CompilerParams(vmem_limit_bytes=limit * 2**20),
        cost_estimate=pl.CostEstimate(flops=flops, bytes_accessed=2**21, transcendentals=0),
    )(*operands)
    return outs if isinstance(out_shape, list) else outs[0]


def send(rows, to):
    pairs = []
    for x in range(X):
        for c in range(C):
            there, core = to(x, c)
            pairs.append((x * C + c, there % X * C + core))
    return lax.ppermute(rows, ("x", "c"), pairs)


def send_home(rows, to):
    pairs = []
    for y in range(Y):
        for x in range(X):
            for c in range(C):
                there, core = to(x, c)
                held = ((y - y % 2 + c) * X + x) * C + y % 2
                pairs.append((held, (y * X + there % X) * C + core))
    return lax.ppermute(rows, ("y", "x", "c"), pairs)


def shards(frames, norm_gain, w_qkv):
    weights = jnp.broadcast_to(jnp.transpose(w_qkv, (1, 0, 2)), (Y, 3, 64, 256))
    weights = lax.all_to_all(weights, "y", 0, 0, tiled=True)
    packed = call(normalize_kernel, (512, 1024), frames, norm_gain.reshape(1, D))
    weights = call(hold_kernel, [weights.shape], weights, packed, in_place=True)[0]
    weights = lax.all_gather(weights, "z", axis=0)
    spread = lax.all_to_all(packed.reshape(64, 8, 1024), ("y", "z"), 0, 0, tiled=True)
    rows = call(merge_kernel, (128, D), spread.reshape(512, 1024))
    place = jnp.stack([lax.axis_index("x"), lax.axis_index("c")]).astype(jnp.int32)
    straight = send_home(rows, lambda x, c: (x + 1 - 2 * c, c))
    crossed = send_home(rows, lambda x, c: (x - 1 + 2 * c, 1 - c))
    own = send_home(rows, lambda x, c: (x, c))
    far = send(straight, lambda x, c: (x + 1 - 2 * c, c))
    swap = lambda part: send(part, lambda x, c: (x, 1 - c))
    held = call(hold_kernel, [crossed.shape], crossed, flops=10**10, in_place=True)[0]
    tokens = (own, swap(own), straight, held, swap(held), swap(straight), far, swap(far))
    mixed = call(
        patches_kernel, (64, 16, 256), place, *tokens, weights, flops=8 * 10**9, far=range(1, 10), limit=44,
        scratch=(VMEM((1024, D), BF), VMEM((Z, Y, 3, 64, 256), BF), pltpu.SemaphoreType.DMA((4, 9))),
    )
    mixed = lax.all_to_all(mixed, ("z", "y"), 0, 0, tiled=True)
    return call(place_kernel, (4, 256, 256), place, mixed)


def solution(mesh):
    grid = Mesh(mesh.devices.reshape(Z, Y, X, C), ("z", "y", "x", "c"))
    rows, columns = ("z", "y"), ("x", "c")
    return jax.shard_map(
        shards, mesh=grid, in_specs=(P(rows, columns, None), P(), P(rows, None, columns)),
        out_specs=P(rows, None, columns), check_vma=False,
    )
```
